32 devices in a mesh: groups: 2 (over y), owner: 16 (over z, x, core).
Axes of the slice: x: 2, y: 2, z: 4, core: 2. Of those that a mesh axis runs over, the one named last changes fastest.
Arguments:
- tokens: bfloat16 [4096, 8192], P(('groups', 'owner')), parts along dimension 0, may hold values from -0.59765625 to 0.59765625
- task_ids: int32 [4096, 1], P(('groups', 'owner')), parts along dimension 0, may hold values from 0 to 15, as said below
- cotangent: bfloat16 [4096, 8192], P(('groups', 'owner')), parts along dimension 0, may hold values from -0.75 to 0.75
- down_factors: bfloat16 [16, 64, 8192], P('owner'), may hold values from -0.75 to 0.75
- up_factors: bfloat16 [16, 64, 8192], P('owner'), may hold values from -0.75 to 0.75
Outputs:
- adapter_out: bfloat16 [4096, 8192], P(('groups', 'owner')), parts along dimension 0
- input_grad: bfloat16 [4096, 8192], P(('groups', 'owner')), parts along dimension 0
- down_grad: bfloat16 [32, 64, 8192], P(('groups', 'owner')), parts along dimension 0
- up_grad: bfloat16 [32, 64, 8192], P(('groups', 'owner')), parts along dimension 0
The draws below stay inside these ranges and needn't reach their ends.
There are 2 independent parts, one for each index of `groups`. The reference program is written for one: setup_inputs(seed, part) draws one part's arguments, and reference() takes and returns one part's arrays. A program takes and returns all parts, laid end to end along the dimension named above; an argument that names none is the same for every part. Nothing has to cross between parts.
Inputs may be any that keep to these rules, and one draw needn't show every extreme that they name: `task_ids`: on every device, one adapter (the same on all devices) has exactly 24 of the device's 128 tokens; every other adapter has at most 8 tokens on a device, and on every device some other adapter has exactly 8.
All inputs are finite; a program needn't handle non-finite values.
Results may differ from the reference program's by a relative error of at most 0.005.
Values may be sent and summed in bfloat16 or wider, within the bound.
A program may use at most 128 MiB of HBM per device.

```python
import jax
import jax.numpy as jnp
from jax import lax

D = 8192
RANK = 64
TOK_DEV = 128
ADAPTERS = 16
TOKENS = 2048
LOW = 8
MOST = 24


def draw_task_ids(key, part):
    key = jax.random.fold_in(key, 7)
    busy_key, rest_key = jax.random.split(key)
    busy_adapter = jax.random.randint(busy_key, (), 0, ADAPTERS).astype(jnp.int32)
    device_keys = jax.random.split(rest_key, ADAPTERS)

    def one_device(device_key):
        order_key, pick_key, place_key = jax.random.split(device_key, 3)
        others = (busy_adapter + 1 + jax.random.permutation(order_key, ADAPTERS - 1).astype(jnp.int32)) % ADAPTERS
        entry_index = jnp.arange((ADAPTERS - 1) * LOW, dtype=jnp.int32)
        entries = others[entry_index // LOW]
        scores = jax.random.permutation(pick_key, (ADAPTERS - 1) * LOW).astype(jnp.int32)
        scores = scores + jnp.where(entry_index < LOW, (ADAPTERS - 1) * LOW, 0).astype(jnp.int32)
        unused, picked = lax.top_k(scores, TOK_DEV - MOST)
        chosen = entries[picked]
        device_tasks = jnp.concatenate([jnp.full((MOST,), busy_adapter, jnp.int32), chosen.astype(jnp.int32)])
        return device_tasks[jax.random.permutation(place_key, TOK_DEV)]
    return jax.vmap(one_device)(device_keys).reshape(TOKENS, 1).astype(jnp.int32)


def steps_of(key, shape, cuts, smallest, high):
    def one(dim, blocks):
        heights = jax.random.uniform(jax.random.fold_in(jax.random.fold_in(key, 6), dim), (blocks,), jnp.float32, smallest / len(cuts), high / len(cuts))
        return jnp.repeat(jnp.exp(heights), shape[dim] // blocks).reshape((-1,) + (1,) * (len(shape) - dim - 1))

    loudness = one(*cuts[0])
    for cut in cuts[1:]:
        loudness = loudness * one(*cut)
    return loudness


def centred(own_key, extent, scale, reach, shards=(), kind=jnp.bfloat16):
    loudness = steps_of(own_key, extent, shards, -0.22, 0.18) if shards else 1.0
    values = jax.random.normal(own_key, extent, jnp.float32) * scale * loudness
    return jnp.minimum(jnp.maximum(values, -reach), reach).astype(kind)


def setup_inputs(seed: int = 0, part: int = 0) -> dict:
    arg_keys = jax.random.split(jax.random.key(seed), 6)
    part_splits = jax.random.split(jax.random.fold_in(arg_keys[5], part), 6)
    return {
        "tokens": centred(part_splits[0], (TOKENS, D), 0.1, 0.59765625, ((0, 16),)),
        "task_ids": draw_task_ids(jax.random.fold_in(jax.random.fold_in(arg_keys[5], part), 71), part),
        "cotangent": centred(part_splits[2], (TOKENS, D), 0.125, 0.75, ((0, 16),)),
        "down_factors": centred(arg_keys[3], (ADAPTERS, RANK, D), 0.125, 0.75, ((0, 16),)),
        "up_factors": centred(arg_keys[4], (ADAPTERS, RANK, D), 0.125, 0.75, ((0, 16),)),
    }


def branch(rows_in, rows_cot, down_mat, up_mat):
    hidden = lax.dot_general(rows_in, down_mat, (((1,), (1,)), ((), ())), preferred_element_type=jnp.float32)
    sig_hidden = jax.nn.sigmoid(hidden)
    activated = (hidden * sig_hidden).astype(jnp.bfloat16)
    result = jnp.dot(activated, up_mat, preferred_element_type=jnp.float32).astype(jnp.bfloat16)
    act_grad = lax.dot_general(rows_cot, up_mat, (((1,), (1,)), ((), ())), preferred_element_type=jnp.float32)
    hid_grad = (act_grad * sig_hidden * (1.0 + hidden * (1.0 - sig_hidden))).astype(jnp.bfloat16)
    in_grad = jnp.dot(hid_grad, down_mat, preferred_element_type=jnp.float32).astype(jnp.bfloat16)
    down_sum = lax.dot_general(hid_grad, rows_in, (((0,), (0,)), ((), ())), preferred_element_type=jnp.float32)
    up_sum = lax.dot_general(activated, rows_cot, (((0,), (0,)), ((), ())), preferred_element_type=jnp.float32)
    return result, in_grad, down_sum, up_sum


def reference(tokens, task_ids, cotangent, down_factors, up_factors):
    task_of = task_ids[:, 0].astype(jnp.int32)
    counts = jnp.bincount(task_of, length=ADAPTERS).astype(jnp.int32)
    sort_order = jnp.argsort(task_of, stable=True).astype(jnp.int32)
    sorted_pos = jnp.zeros((TOKENS,), jnp.int32).at[sort_order].set(jnp.arange(TOKENS, dtype=jnp.int32))
    starts = (jnp.cumsum(counts) - counts).astype(jnp.int32)
    block_count = ((counts + 127) // 128).astype(jnp.int32)
    block_ends = jnp.cumsum(block_count).astype(jnp.int32)
    block_first = (block_ends - block_count).astype(jnp.int32)
    spare_rows = jnp.zeros((128, D), tokens.dtype)
    sorted_in = jnp.concatenate([tokens[sort_order], spare_rows], 0)
    sorted_cot = jnp.concatenate([cotangent[sort_order], spare_rows], 0)

    def per_block(index, state):
        out_main, out_grad, acc_down, acc_up = state
        adapter = jnp.sum((block_ends <= index).astype(jnp.int32)).astype(jnp.int32)
        offset = (starts[adapter] + (index - block_first[adapter]) * 128).astype(jnp.int32)
        live_rows = ((offset + jnp.arange(128, dtype=jnp.int32)) < (starts[adapter] + counts[adapter]))[:, None]
        zero_value = jnp.zeros((), sorted_in.dtype)
        rows_in = jnp.where(live_rows, lax.dynamic_slice_in_dim(sorted_in, offset, 128, 0), zero_value)
        rows_cot = jnp.where(live_rows, lax.dynamic_slice_in_dim(sorted_cot, offset, 128, 0), zero_value)
        result, in_grad, down_sum, up_sum = branch(rows_in, rows_cot, down_factors[adapter], up_factors[adapter])
        old_main = lax.dynamic_slice_in_dim(out_main, offset, 128, 0)
        old_grad = lax.dynamic_slice_in_dim(out_grad, offset, 128, 0)
        out_main = lax.dynamic_update_slice_in_dim(out_main, jnp.where(live_rows, result, old_main), offset, 0)
        out_grad = lax.dynamic_update_slice_in_dim(out_grad, jnp.where(live_rows, in_grad, old_grad), offset, 0)
        acc_down = acc_down.at[adapter].add(down_sum)
        acc_up = acc_up.at[adapter].add(up_sum)
        return out_main, out_grad, acc_down, acc_up

    start_state = (jnp.zeros((TOKENS + 128, D), jnp.bfloat16), jnp.zeros((TOKENS + 128, D), jnp.bfloat16),
                   jnp.zeros((ADAPTERS, RANK, D), jnp.float32), jnp.zeros((ADAPTERS, RANK, D), jnp.float32))
    out_main, out_grad, acc_down, acc_up = lax.fori_loop(jnp.int32(0), block_ends[-1], per_block, start_state)
    adapter_out = out_main[sorted_pos]
    input_grad = out_grad[sorted_pos]
    return adapter_out, input_grad, acc_down.astype(jnp.bfloat16), acc_up.astype(jnp.bfloat16)
```

```python
import jax
import jax.numpy as jnp
from jax import lax
from jax.sharding import PartitionSpec as P

BF = jnp.bfloat16
F32 = jnp.float32


def rows_by_rows(a, b):
    return lax.dot_general(a, b, (((1,), (1,)), ((), ())), preferred_element_type=F32)


def outer_sum(a, b):
    return lax.dot_general(a, b, (((0,), (0,)), ((), ())), preferred_element_type=F32)


def flip(x, bit, owners):
    return lax.ppermute(x, "owner", [(i, i ^ (1 << bit)) for i in range(owners)])


def halve(x, bit, me, owners, wire):
    half = x.shape[0] // 2
    mine = (me >> bit) & 1
    keep = lax.dynamic_slice_in_dim(x, mine * half, half, 0)
    give = lax.dynamic_slice_in_dim(x, (1 - mine) * half, half, 0)
    return keep + flip(give.astype(wire), bit, owners).astype(x.dtype)


def double(x, bit, me, owners):
    other = flip(x, bit, owners)
    mine = (me >> bit) & 1
    low = jnp.where(mine == 0, x, other)
    high = jnp.where(mine == 0, other, x)
    return jnp.concatenate([low, high], 0)


def line_sum(x, me, owners, inner, wire):
    length = owners // inner
    if length == 1:
        return x
    place = me // inner

    def hop(y, moves):
        pairs = [(a * inner + j, b * inner + j) for a, b in moves for j in range(inner)]
        return lax.ppermute(y.astype(wire), "owner", pairs).astype(x.dtype)

    mid = length // 2
    for s in range(mid - 1):
        x = x + hop(x, [(s, s + 1), (length - 1 - s, length - 2 - s)])
    x = x + hop(x, [(mid - 1, mid), (mid, mid - 1)])
    x = x.astype(wire).astype(x.dtype)
    for s in range(mid - 2, -1, -1):
        out = hop(x, [(s + 1, s), (length - 2 - s, length - 1 - s)])
        x = jnp.where((place == s) | (place == length - 1 - s), out, x)
    return x


def sum_over_owner(x, me, owners, wire):
    if owners & (owners - 1) or owners < 8:
        return lax.psum(x, "owner").astype(BF)
    x = halve(x, 0, me, owners, x.dtype)
    x = halve(x, 1, me, owners, wire)
    x = line_sum(x, me, owners, 4, wire).astype(BF)
    x = double(x, 1, me, owners)
    return double(x, 0, me, owners)


def exchange(x, owners):
    y = x.reshape(owners, x.shape[0] // owners, x.shape[1])
    y = lax.all_to_all(y, "owner", split_axis=0, concat_axis=0, tiled=True)
    return y.reshape(x.shape)


def gate(hidden, act_grad):
    sig = jax.nn.sigmoid(hidden)
    activated = (hidden * sig).astype(BF)
    hid_grad = (act_grad * sig * (1.0 + hidden * (1.0 - sig))).astype(BF)
    return activated, hid_grad


def on_device(tokens, task_ids, cotangent, down_factors, up_factors):
    owners = lax.axis_size("owner")
    me = lax.axis_index("owner")
    tok_count, width = tokens.shape
    cold_cap = tok_count // owners
    busy_cap = 3 * cold_cap
    cold_rows = owners * cold_cap
    down_mat = down_factors[0]
    up_mat = up_factors[0]
    rank = down_mat.shape[0]

    task_of = task_ids[:, 0]
    onehot = (task_of[:, None] == jnp.arange(owners, dtype=jnp.int32)[None, :]).astype(BF)
    earlier = jnp.tril(jnp.ones((tok_count, tok_count), BF), -1)
    before = jnp.dot(earlier, onehot, preferred_element_type=F32)
    rank_in = jnp.sum(before * onehot.astype(F32), axis=1).astype(jnp.int32)
    busy = jnp.argmax(jnp.sum(onehot.astype(F32), axis=0)).astype(jnp.int32)
    slot_of = jnp.where(task_of == busy, cold_rows + rank_in, task_of * cold_cap + rank_in)
    slots = jnp.arange(cold_rows + busy_cap, dtype=jnp.int32)
    place = (slots[:, None] == slot_of[None, :]).astype(BF)
    place_cold, place_busy = place[:cold_rows], place[cold_rows:]

    def pick(which, rows):
        return jnp.dot(which, rows, preferred_element_type=F32).astype(BF)

    got_rows = exchange(pick(place_cold, tokens), owners)
    got_cot = exchange(pick(place_cold, cotangent), owners)

    both = jnp.concatenate([down_mat, up_mat], 0)
    both = jnp.where(me == busy, both, jnp.zeros_like(both))
    both = sum_over_owner(both, me, owners, BF)
    busy_down, busy_up = both[:rank], both[rank:]
    busy_rows = pick(place_busy, tokens)
    busy_cot = pick(place_busy, cotangent)
    busy_act, busy_hid = gate(rows_by_rows(busy_rows, busy_down), rows_by_rows(busy_cot, busy_up))
    busy_sums = jnp.concatenate([outer_sum(busy_hid, busy_rows), outer_sum(busy_act, busy_cot)], 0)
    busy_sums = sum_over_owner(busy_sums, me, owners, BF)

    activated, hid_grad = gate(rows_by_rows(got_rows, down_mat), rows_by_rows(got_cot, up_mat))
    back_out = exchange(pick(activated, up_mat), owners)
    back_grad = exchange(pick(hid_grad, down_mat), owners)
    own_sums = jnp.concatenate([outer_sum(hid_grad, got_rows), outer_sum(activated, got_cot)], 0)
    sums = jnp.where(me == busy, busy_sums, own_sums.astype(BF))

    def put(cold, hot):
        cold = outer_sum(place_cold, cold)
        return (cold + outer_sum(place_busy, hot)).astype(BF)

    adapter_out = put(back_out, pick(busy_act, busy_up))
    input_grad = put(back_grad, pick(busy_hid, busy_down))
    return adapter_out, input_grad, sums[:rank][None], sums[rank:][None]


def solution(mesh):
    rows = P(("groups", "owner"), None)
    mats = P(("groups", "owner"), None, None)
    held = P("owner", None, None)
    return jax.shard_map(
        on_device,
        mesh=mesh,
        in_specs=(rows, rows, rows, held, held),
        out_specs=(rows, rows, mats, mats),
        check_vma=False,
    )
```

```python
import jax
import jax.numpy as jnp
from jax import lax
from jax.sharding import PartitionSpec as P

BF = jnp.bfloat16
F32 = jnp.float32


def rows_by_rows(a, b):
    return lax.dot_general(a, b, (((1,), (1,)), ((), ())), preferred_element_type=F32)


def outer_sum(a, b):
    return lax.dot_general(a, b, (((0,), (0,)), ((), ())), preferred_element_type=F32)


def flip(x, bit, owners):
    return lax.ppermute(x, "owner", [(i, i ^ (1 << bit)) for i in range(owners)])


def halve(x, bit, me, owners, wire):
    half = x.shape[0] // 2
    mine = (me >> bit) & 1
    keep = lax.dynamic_slice_in_dim(x, mine * half, half, 0)
    give = lax.dynamic_slice_in_dim(x, (1 - mine) * half, half, 0)
    return keep + flip(give.astype(wire), bit, owners).astype(x.dtype)


def double(x, bit, me, owners):
    other = flip(x, bit, owners)
    mine = (me >> bit) & 1
    low = jnp.where(mine == 0, x, other)
    high = jnp.where(mine == 0, other, x)
    return jnp.concatenate([low, high], 0)


def after(x, other):
    return x + jnp.minimum(jnp.abs(other[0, 0].astype(F32)), 0.0).astype(x.dtype)


def line_sum(x, me, owners, inner, wire, first):
    length = owners // inner
    if length == 1:
        return x
    place = me // inner

    def hop(y, moves):
        pairs = [(a * inner + j, b * inner + j) for a, b in moves for j in range(inner)]
        return lax.ppermute(y.astype(wire), "owner", pairs).astype(x.dtype)

    mid = length // 2
    for s in range(mid - 1):
        x = x + hop(x, [(s, s + 1), (length - 1 - s, length - 2 - s)])
    x = after(x, first)
    x = x + hop(x, [(mid - 1, mid), (mid, mid - 1)])
    x = x.astype(wire).astype(x.dtype)
    for s in range(mid - 2, -1, -1):
        out = hop(x, [(s + 1, s), (length - 2 - s, length - 1 - s)])
        x = jnp.where((place == s) | (place == length - 1 - s), out, x)
    return x


def sum_over_owner(x, me, owners, wire, ties):
    if owners & (owners - 1) or owners < 8:
        return lax.psum(x, "owner").astype(BF)
    middle, third, last = ties
    x = halve(x, 0, me, owners, wire)
    x = halve(x, 1, me, owners, wire)
    x = line_sum(x, me, owners, 4, wire, middle).astype(BF)
    x = double(after(x, third), 1, me, owners)
    return double(after(x, last), 0, me, owners)


def exchange(x, owners):
    y = x.reshape(owners, x.shape[0] // owners, x.shape[1])
    y = lax.all_to_all(y, "owner", split_axis=0, concat_axis=0, tiled=True)
    return y.reshape(x.shape)


def gate(hidden, act_grad):
    sig = jax.nn.sigmoid(hidden)
    activated = (hidden * sig).astype(BF)
    hid_grad = (act_grad * sig * (1.0 + hidden * (1.0 - sig))).astype(BF)
    return activated, hid_grad


def on_device(tokens, task_ids, cotangent, down_factors, up_factors):
    owners = lax.axis_size("owner")
    me = lax.axis_index("owner")
    tok_count, width = tokens.shape
    cold_cap = tok_count // owners
    busy_cap = 3 * cold_cap
    cold_rows = owners * cold_cap
    down_mat = down_factors[0]
    up_mat = up_factors[0]
    rank = down_mat.shape[0]

    task_of = task_ids[:, 0]
    onehot = (task_of[:, None] == jnp.arange(owners, dtype=jnp.int32)[None, :]).astype(BF)
    earlier = jnp.tril(jnp.ones((tok_count, tok_count), BF), -1)
    before = jnp.dot(earlier, onehot, preferred_element_type=F32)
    rank_in = jnp.sum(before * onehot.astype(F32), axis=1).astype(jnp.int32)
    busy = jnp.argmax(jnp.sum(onehot.astype(F32), axis=0)).astype(jnp.int32)
    slot_of = jnp.where(task_of == busy, cold_rows + rank_in, task_of * cold_cap + rank_in)
    slots = jnp.arange(cold_rows + busy_cap, dtype=jnp.int32)
    place = (slots[:, None] == slot_of[None, :]).astype(BF)
    place_cold, place_busy = place[:cold_rows], place[cold_rows:]

    def pick(which, rows):
        return jnp.dot(which, rows, preferred_element_type=F32).astype(BF)

    got_rows = exchange(pick(place_cold, tokens), owners)
    got_cot = exchange(pick(place_cold, cotangent), owners)

    activated, hid_grad = gate(rows_by_rows(got_rows, down_mat), rows_by_rows(got_cot, up_mat))
    back_out = exchange(pick(activated, up_mat), owners)
    back_grad = exchange(pick(hid_grad, down_mat), owners)
    own_sums = jnp.concatenate([outer_sum(hid_grad, got_rows), outer_sum(activated, got_cot)], 0)

    both = jnp.concatenate([down_mat, up_mat], 0)
    both = jnp.where(me == busy, both, jnp.zeros_like(both))
    both = sum_over_owner(both, me, owners, BF, (got_rows, got_cot, back_out))
    busy_down, busy_up = both[:rank], both[rank:]
    busy_rows = pick(place_busy, tokens)
    busy_cot = pick(place_busy, cotangent)
    busy_act, busy_hid = gate(rows_by_rows(busy_rows, busy_down), rows_by_rows(busy_cot, busy_up))
    busy_sums = jnp.concatenate([outer_sum(busy_hid, busy_rows), outer_sum(busy_act, busy_cot)], 0)

    def put(cold, hot):
        cold = outer_sum(place_cold, cold)
        return (cold + outer_sum(place_busy, hot)).astype(BF)

    adapter_out = put(back_out, pick(busy_act, busy_up))
    input_grad = put(back_grad, pick(busy_hid, busy_down))
    busy_sums = sum_over_owner(busy_sums, me, owners, BF, (back_grad, adapter_out, input_grad))
    sums = jnp.where(me == busy, busy_sums, own_sums.astype(BF))
    return adapter_out, input_grad, sums[:rank][None], sums[rank:][None]


def solution(mesh):
    rows = P(("groups", "owner"), None)
    mats = P(("groups", "owner"), None, None)
    held = P("owner", None, None)
    return jax.shard_map(
        on_device,
        mesh=mesh,
        in_specs=(rows, rows, rows, held, held),
        out_specs=(rows, rows, mats, mats),
        check_vma=False,
    )
```

```python
import jax
import jax.numpy as jnp
from jax import lax
from jax.sharding import PartitionSpec as P

BF = jnp.bfloat16
F32 = jnp.float32


def rows_by_rows(a, b):
    return lax.dot_general(a, b, (((1,), (1,)), ((), ())), preferred_element_type=F32)


def outer_sum(a, b):
    return lax.dot_general(a, b, (((0,), (0,)), ((), ())), preferred_element_type=F32)


def flip(x, bit, owners):
    return lax.ppermute(x, "owner", [(i, i ^ (1 << bit)) for i in range(owners)])


def halve(x, bit, me, owners, wire):
    half = x.shape[0] // 2
    mine = (me >> bit) & 1
    keep = lax.dynamic_slice_in_dim(x, mine * half, half, 0)
    give = lax.dynamic_slice_in_dim(x, (1 - mine) * half, half, 0)
    return keep + flip(give.astype(wire), bit, owners).astype(x.dtype)


def double(x, bit, me, owners):
    other = flip(x, bit, owners)
    mine = (me >> bit) & 1
    low = jnp.where(mine == 0, x, other)
    high = jnp.where(mine == 0, other, x)
    return jnp.concatenate([low, high], 0)


def after(x, other):
    return x + jnp.minimum(jnp.abs(other[0, 0].astype(F32)), 0.0).astype(x.dtype)


def line_sum(x, me, owners, inner, wire, first):
    length = owners // inner
    if length == 1:
        return x
    place = me // inner

    def hop(y, moves):
        pairs = [(a * inner + j, b * inner + j) for a, b in moves for j in range(inner)]
        return lax.ppermute(y.astype(wire), "owner", pairs).astype(x.dtype)

    mid = length // 2
    for s in range(mid - 1):
        x = x + hop(x, [(s, s + 1), (length - 1 - s, length - 2 - s)])
    x = after(x, first)
    x = x + hop(x, [(mid - 1, mid), (mid, mid - 1)])
    x = x.astype(wire).astype(x.dtype)
    for s in range(mid - 2, -1, -1):
        out = hop(x, [(s + 1, s), (length - 2 - s, length - 1 - s)])
        x = jnp.where((place == s) | (place == length - 1 - s), out, x)
    return x


def sum_over_owner(x, me, owners, wire, ties):
    if owners & (owners - 1) or owners < 8:
        return lax.psum(x, "owner").astype(BF)
    middle, third, last, final = ties
    x = halve(x, 0, me, owners, wire)
    x = halve(x, 1, me, owners, wire)
    x = line_sum(x, me, owners, 4, wire, middle).astype(BF)
    x = double(after(after(x, third), last), 1, me, owners)
    return double(after(x, final), 0, me, owners)


def exchange(x, owners):
    y = x.reshape(owners, x.shape[0] // owners, x.shape[1])
    y = lax.all_to_all(y, "owner", split_axis=0, concat_axis=0, tiled=True)
    return y.reshape(x.shape)


def gate(hidden, act_grad):
    sig = jax.nn.sigmoid(hidden)
    activated = (hidden * sig).astype(BF)
    hid_grad = (act_grad * sig * (1.0 + hidden * (1.0 - sig))).astype(BF)
    return activated, hid_grad


def on_device(tokens, task_ids, cotangent, down_factors, up_factors):
    owners = lax.axis_size("owner")
    me = lax.axis_index("owner")
    tok_count, width = tokens.shape
    cold_cap = tok_count // owners
    busy_cap = 3 * cold_cap
    cold_rows = owners * cold_cap
    down_mat = down_factors[0]
    up_mat = up_factors[0]
    rank = down_mat.shape[0]

    task_of = task_ids[:, 0]
    onehot = (task_of[:, None] == jnp.arange(owners, dtype=jnp.int32)[None, :]).astype(BF)
    earlier = jnp.tril(jnp.ones((tok_count, tok_count), BF), -1)
    before = jnp.dot(earlier, onehot, preferred_element_type=F32)
    rank_in = jnp.sum(before * onehot.astype(F32), axis=1).astype(jnp.int32)
    busy = jnp.argmax(jnp.sum(onehot.astype(F32), axis=0)).astype(jnp.int32)
    slot_of = jnp.where(task_of == busy, cold_rows + rank_in, task_of * cold_cap + rank_in)
    slots = jnp.arange(cold_rows + busy_cap, dtype=jnp.int32)
    place = (slots[:, None] == slot_of[None, :]).astype(BF)
    place_cold, place_busy = place[:cold_rows], place[cold_rows:]

    def pick(which, rows):
        return jnp.dot(which, rows, preferred_element_type=F32).astype(BF)

    got_rows = exchange(pick(place_cold, tokens), owners)
    got_cot = exchange(pick(place_cold, cotangent), owners)

    activated, hid_grad = gate(rows_by_rows(got_rows, down_mat), rows_by_rows(got_cot, up_mat))
    back_out = exchange(pick(activated, up_mat), owners)
    back_grad = exchange(pick(hid_grad, down_mat), owners)
    own_sums = jnp.concatenate([outer_sum(hid_grad, got_rows), outer_sum(activated, got_cot)], 0).astype(BF)

    both = jnp.concatenate([down_mat, up_mat], 0)
    both = jnp.where(me == busy, both, jnp.zeros_like(both))
    both = sum_over_owner(both, me, owners, BF, (got_rows, got_cot, got_cot, back_out))
    busy_down, busy_up = both[:rank], both[rank:]
    busy_rows = pick(place_busy, tokens)
    busy_cot = pick(place_busy, cotangent)
    busy_act, busy_hid = gate(rows_by_rows(busy_rows, busy_down), rows_by_rows(busy_cot, busy_up))
    busy_sums = jnp.concatenate([outer_sum(busy_hid, busy_rows), outer_sum(busy_act, busy_cot)], 0)

    def put(cold, hot):
        cold = outer_sum(place_cold, cold)
        return (cold + outer_sum(place_busy, hot)).astype(BF)

    adapter_out = put(back_out, pick(busy_act, busy_up))
    input_grad = put(back_grad, pick(busy_hid, busy_down))
    busy_sums = sum_over_owner(busy_sums, me, owners, BF, (back_grad, input_grad, adapter_out, own_sums))
    sums = jnp.where(me == busy, busy_sums, own_sums)
    return adapter_out, input_grad, sums[:rank][None], sums[rank:][None]


def solution(mesh):
    rows = P(("groups", "owner"), None)
    mats = P(("groups", "owner"), None, None)
    held = P("owner", None, None)
    return jax.shard_map(
        on_device,
        mesh=mesh,
        in_specs=(rows, rows, rows, held, held),
        out_specs=(rows, rows, mats, mats),
        check_vma=False,
    )
```

```python
import jax
import jax.numpy as jnp
from jax import lax
from jax.sharding import PartitionSpec as P

BF = jnp.bfloat16
F32 = jnp.float32


def rows_by_rows(a, b):
    return lax.dot_general(a, b, (((1,), (1,)), ((), ())), preferred_element_type=F32)


def outer_sum(a, b):
    return lax.dot_general(a, b, (((0,), (0,)), ((), ())), preferred_element_type=F32)


def flip(x, bit, owners):
    return lax.ppermute(x, "owner", [(i, i ^ (1 << bit)) for i in range(owners)])


def halve(x, bit, me, owners, wire):
    half = x.shape[0] // 2
    mine = (me >> bit) & 1
    keep = lax.dynamic_slice_in_dim(x, mine * half, half, 0)
    give = lax.dynamic_slice_in_dim(x, (1 - mine) * half, half, 0)
    return keep + flip(give.astype(wire), bit, owners).astype(x.dtype)


def double(x, bit, me, owners):
    other = flip(x, bit, owners)
    mine = (me >> bit) & 1
    low = jnp.where(mine == 0, x, other)
    high = jnp.where(mine == 0, other, x)
    return jnp.concatenate([low, high], 0)


def after(x, other):
    return x + jnp.minimum(jnp.abs(other[0, 0].astype(F32)), 0.0).astype(x.dtype)


def line_sum(x, me, owners, inner, wire, first):
    length = owners // inner
    if length == 1:
        return x
    place = me // inner

    def hop(y, moves):
        pairs = [(a * inner + j, b * inner + j) for a, b in moves for j in range(inner)]
        return lax.ppermute(y.astype(wire), "owner", pairs).astype(x.dtype)

    mid = length // 2
    for s in range(mid - 1):
        x = x + hop(x, [(s, s + 1), (length - 1 - s, length - 2 - s)])
    x = after(x, first)
    x = x + hop(x, [(mid - 1, mid), (mid, mid - 1)])
    x = x.astype(wire).astype(x.dtype)
    for s in range(mid - 2, -1, -1):
        out = hop(x, [(s + 1, s), (length - 2 - s, length - 1 - s)])
        x = jnp.where((place == s) | (place == length - 1 - s), out, x)
    return x


def sum_over_owner(x, me, owners, wire, ties):
    if owners & (owners - 1) or owners < 8:
        return lax.psum(x, "owner").astype(BF)
    middle, third, final = ties
    x = halve(x, 0, me, owners, wire)
    x = halve(x, 1, me, owners, wire)
    x = line_sum(x, me, owners, 4, wire, middle).astype(BF)
    for other in third:
        x = after(x, other)
    x = double(x, 1, me, owners)
    return double(after(x, final), 0, me, owners)


def exchange(x, owners):
    y = x.reshape(owners, x.shape[0] // owners, x.shape[1])
    y = lax.all_to_all(y, "owner", split_axis=0, concat_axis=0, tiled=True)
    return y.reshape(x.shape)


def gate(hidden, act_grad):
    sig = jax.nn.sigmoid(hidden)
    activated = (hidden * sig).astype(BF)
    hid_grad = (act_grad * sig * (1.0 + hidden * (1.0 - sig))).astype(BF)
    return activated, hid_grad


def on_device(tokens, task_ids, cotangent, down_factors, up_factors):
    owners = lax.axis_size("owner")
    me = lax.axis_index("owner")
    tok_count, width = tokens.shape
    cold_cap = tok_count // owners
    busy_cap = 3 * cold_cap
    cold_rows = owners * cold_cap
    down_mat = down_factors[0]
    up_mat = up_factors[0]
    rank = down_mat.shape[0]

    task_of = task_ids[:, 0]
    onehot = (task_of[:, None] == jnp.arange(owners, dtype=jnp.int32)[None, :]).astype(BF)
    earlier = jnp.tril(jnp.ones((tok_count, tok_count), BF), -1)
    before = jnp.dot(earlier, onehot, preferred_element_type=F32)
    rank_in = jnp.sum(before * onehot.astype(F32), axis=1).astype(jnp.int32)
    busy = jnp.argmax(jnp.sum(onehot.astype(F32), axis=0)).astype(jnp.int32)
    slot_of = jnp.where(task_of == busy, cold_rows + rank_in, task_of * cold_cap + rank_in)
    slots = jnp.arange(cold_rows + busy_cap, dtype=jnp.int32)
    place = (slots[:, None] == slot_of[None, :]).astype(BF)
    place_cold, place_busy = place[:cold_rows], place[cold_rows:]

    def pick(which, rows):
        return jnp.dot(which, rows, preferred_element_type=F32).astype(BF)

    got_rows = exchange(pick(place_cold, tokens), owners)
    got_cot = exchange(pick(place_cold, cotangent), owners)

    activated, hid_grad = gate(rows_by_rows(got_rows, down_mat), rows_by_rows(got_cot, up_mat))
    back_out = exchange(pick(activated, up_mat), owners)
    back_grad = exchange(pick(hid_grad, down_mat), owners)
    own_down = outer_sum(hid_grad, got_rows).astype(BF)
    own_up = outer_sum(activated, got_cot).astype(BF)

    both = jnp.concatenate([down_mat, up_mat], 0)
    both = jnp.where(me == busy, both, jnp.zeros_like(both))
    both = sum_over_owner(both, me, owners, BF, (got_rows, (got_cot,), back_out))
    busy_down, busy_up = both[:rank], both[rank:]
    busy_rows = pick(place_busy, tokens)
    busy_cot = pick(place_busy, cotangent)
    busy_act, busy_hid = gate(rows_by_rows(busy_rows, busy_down), rows_by_rows(busy_cot, busy_up))
    busy_sums = jnp.concatenate([outer_sum(busy_hid, busy_rows), outer_sum(busy_act, busy_cot)], 0)

    def put(cold, hot):
        cold = outer_sum(place_cold, cold)
        return (cold + outer_sum(place_busy, hot)).astype(BF)

    adapter_out = put(back_out, pick(busy_act, busy_up))
    input_grad = put(back_grad, pick(busy_hid, busy_down))
    busy_sums = sum_over_owner(busy_sums, me, owners, BF, (back_grad, (input_grad, adapter_out, own_down, own_up), own_up))
    down_sum = jnp.where(me == busy, busy_sums[:rank], own_down)
    up_sum = jnp.where(me == busy, busy_sums[rank:], own_up)
    return adapter_out, input_grad, down_sum[None], up_sum[None]


def solution(mesh):
    rows = P(("groups", "owner"), None)
    mats = P(("groups", "owner"), None, None)
    held = P("owner", None, None)
    return jax.shard_map(
        on_device,
        mesh=mesh,
        in_specs=(rows, rows, rows, held, held),
        out_specs=(rows, rows, mats, mats),
        check_vma=False,
    )
```
